32 devices in a mesh: state: 8 (over z, x), basis: 4 (over y, core).
Axes of the slice: x: 2, y: 2, z: 4, core: 2. Of those that a mesh axis runs over, the one named last changes fastest.
Arguments:
- lower_vectors: bfloat16 [61440, 3072], P('basis', 'state'), may hold values from -6 to 6
- upper_vectors: bfloat16 [61440, 2048], P('basis', 'state'), may hold values from -6 to 6
- lower_labels: int32 [3072], P('state'), may hold values from 0 to 3
- upper_labels: int32 [2048], P('state'), may hold values from 0 to 3
- band_offsets: int32 [960], P('basis'), may hold values from -2 to 2
- dipole_blocks: bfloat16 [960, 64, 128], P('basis'), may hold values from -0.5 to 0.5
- pair_table: int32 [4, 4], replicated, may hold values 0 or 1
Outputs:
- moments: float32 [3072, 1024], P('state', 'basis')
The draws below stay inside these ranges and needn't reach their ends.
All inputs are finite; a program needn't handle non-finite values.
Results may differ from the reference program's by a relative error of at most 0.0029.
Values may be sent and summed in bfloat16 or wider, within the bound.
A program may use at most 128 MiB of HBM per device.

```python
import jax
import jax.numpy as jnp
from jax import lax

BASIS = 61440
BLK = 64
NSYM = 4
STEPS = 4
LOW_DEV = 384
UP_DEV = 256
NBLOCKS = 960
LOWER = 3072
UPPER = 2048
N_STATE = 8


def touch_ends(entries, key, smallest, largest):
    shape = entries.shape
    spot = [jax.random.randint(jax.random.fold_in(key, axis), (), 0, shape[axis]) for axis in range(len(shape))]
    entries = entries.at[tuple(spot)].set(smallest)
    longest = shape.index(max(shape))
    spot[longest] = (spot[longest] + 1) % shape[longest]
    return entries.at[tuple(spot)].set(largest)


def block_levels(own_key, shape, pieces, smallest, top_value):
    level, own = 1.0, jax.random.fold_in(own_key, 6)
    for dim, blocks in pieces:
        heights = jnp.exp(jax.random.uniform(jax.random.fold_in(own, dim), (blocks,), jnp.float32, smallest / len(pieces), top_value / len(pieces)))
        level = level * jnp.repeat(heights, shape[dim] // blocks).reshape([-1 if axis == dim else 1 for axis in range(len(shape))])
    return level


def noise(own_key, extent, width, limit, pieces=(), kind=jnp.bfloat16):
    level = block_levels(own_key, extent, pieces, -0.22, 0.18) if pieces else 1.0
    values = jax.random.normal(own_key, extent, jnp.float32) * width * level
    return jnp.minimum(jnp.maximum(values, -limit), limit).astype(kind)


def setup_inputs(seed: int = 0) -> dict:
    key_list = jax.random.split(jax.random.key(seed), 8)
    return {
        "lower_vectors": noise(key_list[0], (BASIS, LOWER), 1.0, 6.0, ((0, 4), (1, 8))),
        "upper_vectors": noise(key_list[1], (BASIS, UPPER), 1.0, 6.0, ((0, 4), (1, 8))),
        "lower_labels": touch_ends(jax.random.randint(key_list[2], (LOWER,), 0, NSYM), jax.random.fold_in(key_list[2], 1), 0, NSYM - 1).astype(jnp.int32),
        "upper_labels": touch_ends(jax.random.randint(key_list[3], (UPPER,), 0, NSYM), jax.random.fold_in(key_list[3], 1), 0, NSYM - 1).astype(jnp.int32),
        "band_offsets": touch_ends(jax.random.randint(key_list[4], (NBLOCKS,), -2, 3), jax.random.fold_in(key_list[4], 1), -2, 2).astype(jnp.int32),
        "dipole_blocks": noise(key_list[5], (NBLOCKS, BLK, 2 * BLK), (2 * BLK) ** -0.5, 0.5, ((0, 4),)),
        "pair_table": touch_ends((jax.random.randint(key_list[6], (NSYM, NSYM), 0, 3) < 2).astype(jnp.int32), jax.random.fold_in(key_list[6], 1), 0, 1),
    }


def image_blocks(upper_vectors, band_offsets, dipole_blocks):
    padded = jnp.pad(upper_vectors, ((2 * BLK, 2 * BLK), (0, 0)))
    blocks = padded.reshape(NBLOCKS + 4, BLK, UPPER)

    def one_block(number):
        own_block = blocks[number + 2]
        coupled = blocks[number + 2 + band_offsets[number]]
        stacked = jnp.concatenate([own_block, coupled], axis=0)
        return jnp.dot(dipole_blocks[number], stacked, preferred_element_type=jnp.float32).astype(jnp.bfloat16)

    return lax.map(one_block, jnp.arange(NBLOCKS, dtype=jnp.int32)).reshape(BASIS, UPPER)


def reference(lower_vectors, upper_vectors, lower_labels, upper_labels, band_offsets, dipole_blocks, pair_table):
    dipole_image = image_blocks(upper_vectors, band_offsets, dipole_blocks)
    norm_scale = float(BASIS) ** -0.5

    def one_state(state):
        first_lower = (state * LOW_DEV).astype(jnp.int32)
        lower_block = lax.dynamic_slice_in_dim(lower_vectors, first_lower, LOW_DEV, 1)
        labels_lower = lax.dynamic_slice_in_dim(lower_labels, first_lower, LOW_DEV, 0)
        columns = []
        for cycle_step in range(STEPS):
            source = (((state - cycle_step) % N_STATE) * UP_DEV).astype(jnp.int32)
            image_block = lax.dynamic_slice_in_dim(dipole_image, source, UP_DEV, 1)
            labels_upper = lax.dynamic_slice_in_dim(upper_labels, source, UP_DEV, 0)
            allowed = pair_table[labels_lower[:, None], labels_upper[None, :]].astype(jnp.float32)
            product = lax.dot_general(lower_block, image_block, (((0,), (0,)), ((), ())), preferred_element_type=jnp.float32)
            columns.append(product * allowed * norm_scale)
        return jnp.stack(columns, axis=2).reshape(LOW_DEV, UP_DEV * STEPS)

    result = lax.map(one_state, jnp.arange(N_STATE, dtype=jnp.int32))
    return result.reshape(N_STATE * LOW_DEV, UP_DEV * STEPS)
```

```python
import functools

import jax
import jax.numpy as jnp
from jax import lax
from jax.experimental import pallas as pl
from jax.experimental.pallas import tpu as pltpu
from jax.sharding import PartitionSpec as P

STEPS = 4
CHUNK = 512
AHEAD = 3
MESH = pl.DeviceIdType.MESH


def kernel(
    states,
    parts,
    chunks,
    block_size,
    offsets,
    low,
    high,
    upper_hbm,
    dipole,
    lower_hbm,
    out,
    upper,
    own,
    from_two,
    from_one,
    from_three,
    passing,
    lower,
    totals,
    load_sem,
    lower_sem,
    two_sem,
    one_sem,
    three_sem,
    passing_sem,
    send_up,
    send_across,
    send_swap,
    send_second,
    send_passing,
    send_last,
):
    me = lax.axis_index("state")
    odd = lax.rem(me, 2)
    is_odd = odd == 1
    is_even = odd == 0
    partner = me + 1 - 2 * odd
    above = lax.rem(me + 2, states)
    below = lax.rem(me + states - 2, states)
    blocks = upper_hbm.shape[0]
    per_chunk = CHUNK // block_size

    load = pltpu.make_async_copy(upper_hbm, upper.at[pl.ds(2, blocks)], load_sem)
    load.start()
    barrier = pltpu.get_barrier_semaphore()
    for other in (partner, above, below):
        pl.semaphore_signal(barrier, inc=1, device_id={"state": other}, device_id_type=MESH)
    upper[pl.ds(0, 2)] = low[...]
    upper[pl.ds(2 + blocks, 2)] = high[...]
    totals[...] = jnp.zeros_like(totals)
    load.wait()
    pl.semaphore_wait(barrier, 3)

    def copy(source, target, send, receive, device):
        return pltpu.make_async_remote_copy(
            src_ref=source,
            dst_ref=target,
            send_sem=send,
            recv_sem=receive,
            device_id={"state": device},
            device_id_type=MESH,
        )

    def up(c):
        return copy(own.at[c], from_two.at[c], send_up.at[c], two_sem.at[c], above)

    def across(c):
        return copy(own.at[c], from_one.at[c], send_across.at[c], one_sem.at[c], partner)

    def swap_odd(c):
        return copy(from_two.at[c], from_one.at[c], send_swap.at[c], one_sem.at[c], partner)

    def swap_even(c):
        return copy(from_two.at[c], from_three.at[c], send_swap.at[c], three_sem.at[c], partner)

    def second(c):
        return copy(from_one.at[c], from_three.at[c], send_second.at[c], three_sem.at[c], above)

    def passed(c):
        g = c // 3
        return copy(from_two.at[c], passing.at[g], send_passing.at[g], passing_sem.at[g], above)

    def last(c):
        g = c // 3
        return copy(passing.at[g], from_three.at[c], send_last.at[g], three_sem.at[c], partner)

    def make_image(c):
        for j in range(per_chunk):
            b = c * per_chunk + j
            stacked = jnp.concatenate([upper[b + 2], upper[b + 2 + offsets[b]]], axis=0)
            block = jnp.dot(dipole[b], stacked, preferred_element_type=jnp.float32)
            own[c, pl.ds(j * block_size, block_size), :] = block.astype(jnp.bfloat16)

    def body(t, carry):
        @pl.when(t < chunks)
        def _():
            make_image(t)
            up(t).start()

            @pl.when(is_even)
            def _():
                across(t).start()

        c = t - AHEAD

        @pl.when((c >= 0) & (c < chunks))
        def _():
            kind = lax.rem(c, 3)
            up(c).wait_recv()

            @pl.when(is_odd)
            def _():
                swap_odd(c).start()

            @pl.when(is_odd & (kind == 2))
            def _():
                passed(c).start()

            @pl.when(is_even & (kind != 0))
            def _():
                swap_even(c).start()

        b = t - AHEAD - 1

        @pl.when((b >= 0) & (b < chunks))
        def _():
            kind = lax.rem(b, 3)
            across(b).wait_recv()

            @pl.when((kind == 0) | (is_even & (kind == 1)))
            def _():
                second(b).start()

        e = t - AHEAD - 2

        @pl.when((e >= 0) & (e < chunks) & is_odd & (lax.rem(e, 3) == 2))
        def _():
            passed(e).wait_recv()
            last(e).start()

        h = t - AHEAD - 3

        @pl.when((h >= 0) & (h < chunks))
        def _():
            first = pl.multiple_of(h * CHUNK, CHUNK)
            fetch = pltpu.make_async_copy(lower_hbm.at[pl.ds(first, CHUNK)], lower, lower_sem)
            fetch.start()
            second(h).wait_recv()
            fetch.wait()
            for k, held in enumerate((own, from_one, from_two, from_three)):
                totals[k] += lax.dot_general(
                    held[h], lower[...], (((0,), (0,)), ((), ())), preferred_element_type=jnp.float32
                )

        return carry

    lax.fori_loop(0, chunks + AHEAD + 3, body, 0)

    def drain(c, carry):
        kind = lax.rem(c, 3)
        up(c).wait_send()

        @pl.when(is_even)
        def _():
            across(c).wait_send()

        @pl.when(is_odd)
        def _():
            swap_odd(c).wait_send()

        @pl.when(is_odd & (kind == 2))
        def _():
            passed(c).wait_send()
            last(c).wait_send()

        @pl.when(is_even & (kind != 0))
        def _():
            swap_even(c).wait_send()

        @pl.when((kind == 0) | (is_even & (kind == 1)))
        def _():
            second(c).wait_send()

        return carry

    lax.fori_loop(0, chunks, drain, 0)
    share = totals.shape[1] // parts
    for p in range(parts):
        for k in range(STEPS):
            out[pl.ds((p * STEPS + k) * share, share), :] = totals[k, pl.ds(p * share, share), :]


def partial_moments(states, parts, offsets, low, high, upper_vectors, dipole_blocks, lower_vectors):
    rows, upper_count = upper_vectors.shape
    lower_count = lower_vectors.shape[1]
    block_size = dipole_blocks.shape[1]
    chunks = rows // CHUNK
    groups = (chunks + 2) // 3
    held = pltpu.VMEM((chunks, CHUNK, upper_count), jnp.bfloat16)
    vmem = pl.BlockSpec(memory_space=pltpu.VMEM)
    hbm = pl.BlockSpec(memory_space=pl.ANY)
    dma = pltpu.SemaphoreType.DMA
    return pl.pallas_call(
        functools.partial(kernel, states, parts, chunks, block_size),
        out_shape=jax.ShapeDtypeStruct((upper_count * STEPS, lower_count), jnp.float32),
        in_specs=[pl.BlockSpec(memory_space=pltpu.SMEM), vmem, vmem, hbm, vmem, hbm],
        out_specs=vmem,
        scratch_shapes=[
            pltpu.VMEM((rows // block_size + 4, block_size, upper_count), jnp.bfloat16),
            held,
            held,
            held,
            held,
            pltpu.VMEM((groups, CHUNK, upper_count), jnp.bfloat16),
            pltpu.VMEM((CHUNK, lower_count), jnp.bfloat16),
            pltpu.VMEM((STEPS, upper_count, lower_count), jnp.float32),
            dma,
            dma,
            dma((chunks,)),
            dma((chunks,)),
            dma((chunks,)),
            dma((groups,)),
            dma((chunks,)),
            dma((chunks,)),
            dma((chunks,)),
            dma((chunks,)),
            dma((groups,)),
            dma((groups,)),
        ],
        compiler_params=pltpu.CompilerParams(
            collective_id=0, has_side_effects=True, vmem_limit_bytes=58 * 1024 * 1024
        ),
        cost_estimate=pl.CostEstimate(
            flops=2 * rows * upper_count * (STEPS * lower_count + 2 * block_size),
            bytes_accessed=2 * rows * (upper_count + lower_count + 2 * block_size),
            transcendentals=0,
        ),
    )(
        offsets,
        low.reshape(2, block_size, upper_count),
        high.reshape(2, block_size, upper_count),
        upper_vectors.reshape(-1, block_size, upper_count),
        dipole_blocks,
        lower_vectors,
    )


def halos(block, width):
    count = lax.axis_size("basis")
    forward = [(i, i + 1) for i in range(count - 1)]
    backward = [(target, source) for source, target in forward]
    low = lax.ppermute(lax.slice_in_dim(block, block.shape[0] - width, None, axis=0), "basis", forward)
    high = lax.ppermute(lax.slice_in_dim(block, 0, width, axis=0), "basis", backward)
    return low, high


def window_labels(upper_labels):
    count = lax.axis_size("state")
    windows = [upper_labels]
    for k in range(1, STEPS):
        pairs = [(source, (source + k) % count) for source in range(count)]
        windows.append(lax.ppermute(upper_labels, "state", pairs))
    return jnp.stack(windows, axis=1).reshape(-1)


def local(
    lower_vectors,
    upper_vectors,
    lower_labels,
    upper_labels,
    band_offsets,
    dipole_blocks,
    pair_table,
):
    states = lax.axis_size("state")
    basis = lax.axis_size("basis")
    low, high = halos(upper_vectors, 2 * dipole_blocks.shape[1])
    partial = partial_moments(
        states, basis, band_offsets, low, high, upper_vectors, dipole_blocks, lower_vectors
    )
    summed = lax.psum_scatter(partial, "basis", scatter_dimension=0, tiled=True)
    labels = window_labels(upper_labels)
    share = labels.shape[0] // basis
    labels = lax.dynamic_slice_in_dim(labels, lax.axis_index("basis") * share, share, 0)
    symbols = jnp.arange(pair_table.shape[0], dtype=jnp.int32)
    lower_onehot = (lower_labels[:, None] == symbols[None, :]).astype(jnp.float32)
    upper_onehot = (labels[:, None] == symbols[None, :]).astype(jnp.float32)
    allowed = jnp.dot(
        jnp.dot(lower_onehot, pair_table.astype(jnp.float32), precision=lax.Precision.HIGHEST),
        upper_onehot.T,
        precision=lax.Precision.HIGHEST,
    )
    norm_scale = float(lower_vectors.shape[0] * basis) ** (-0.5)
    summed = summed.reshape(STEPS, -1, summed.shape[1]).transpose(2, 1, 0)
    return summed.reshape(allowed.shape) * allowed * norm_scale


def solution(mesh):
    return jax.shard_map(
        local,
        mesh=mesh,
        in_specs=(
            P("basis", "state"),
            P("basis", "state"),
            P("state"),
            P("state"),
            P("basis"),
            P("basis", None, None),
            P(),
        ),
        out_specs=P("state", "basis"),
        check_vma=False,
    )
```

```python
import functools

import jax
import jax.numpy as jnp
from jax import lax
from jax.experimental import pallas as pl
from jax.experimental.pallas import tpu as pltpu
from jax.sharding import PartitionSpec as P

STEPS = 4
CHUNK = 512
AHEAD = 2
MESH = pl.DeviceIdType.MESH


def kernel(
    states,
    parts,
    chunks,
    block_size,
    offsets,
    labels,
    upper_hbm,
    dipole,
    lower_hbm,
    out,
    labels_out,
    upper,
    own,
    from_two,
    from_one,
    from_three,
    passing,
    lower,
    totals,
    load_sem,
    lower_sem,
    two_sem,
    one_sem,
    three_sem,
    passing_sem,
    send_up,
    send_across,
    send_swap,
    send_second,
    send_passing,
    send_last,
    windows,
    near,
    far,
    label_send,
    label_sem,
    halo_send,
    halo_sem,
    near_send,
    near_sem,
    far_send,
    far_sem,
):
    me = lax.axis_index("state")
    odd = lax.rem(me, 2)
    is_odd = odd == 1
    is_even = odd == 0
    partner = me + 1 - 2 * odd
    above = lax.rem(me + 2, states)
    below = lax.rem(me + states - 2, states)
    blocks = upper_hbm.shape[0]
    per_chunk = CHUNK // block_size

    part = lax.axis_index("basis")
    core = lax.rem(part, 2)
    place = part // 2
    places = parts // 2

    load = pltpu.make_async_copy(upper_hbm, upper.at[pl.ds(2, blocks)], load_sem)
    load.start()
    barrier = pltpu.get_barrier_semaphore()
    for step in range(1, STEPS):
        for other in (lax.rem(me + step, states), lax.rem(me + states - step, states)):
            pl.semaphore_signal(barrier, inc=1, device_id={"state": other}, device_id_type=MESH)
    for step in range(1, parts):
        other = lax.rem(part + step, parts)
        pl.semaphore_signal(barrier, inc=1, device_id={"basis": other}, device_id_type=MESH)
    edge = jnp.zeros((2,) + upper.shape[1:], upper.dtype)

    @pl.when(part == 0)
    def _():
        upper[pl.ds(0, 2)] = edge

    @pl.when(part == parts - 1)
    def _():
        upper[pl.ds(2 + blocks, 2)] = edge

    totals[...] = jnp.zeros_like(totals)
    pl.semaphore_wait(barrier, 2 * (STEPS - 1) + parts - 1)

    def along(source, target, send, receive, device):
        return pltpu.make_async_remote_copy(
            src_ref=source,
            dst_ref=target,
            send_sem=send,
            recv_sem=receive,
            device_id={"basis": device},
            device_id_type=MESH,
        )

    to_next = along(
        upper_hbm.at[pl.ds(blocks - 2, 2)],
        upper.at[pl.ds(0, 2)],
        halo_send.at[0],
        halo_sem.at[0],
        lax.rem(part + 1, parts),
    )
    to_last = along(
        upper_hbm.at[pl.ds(0, 2)],
        upper.at[pl.ds(2 + blocks, 2)],
        halo_send.at[1],
        halo_sem.at[1],
        lax.rem(part + parts - 1, parts),
    )

    @pl.when(part < parts - 1)
    def _():
        to_next.start()

    @pl.when(part > 0)
    def _():
        to_last.start()

    def copy(source, target, send, receive, device):
        return pltpu.make_async_remote_copy(
            src_ref=source,
            dst_ref=target,
            send_sem=send,
            recv_sem=receive,
            device_id={"state": device},
            device_id_type=MESH,
        )

    def window(k):
        return copy(
            labels,
            windows.at[k - 1],
            label_send.at[k - 1],
            label_sem.at[k - 1],
            lax.rem(me + k, states),
        )

    for k in range(1, STEPS):
        window(k).start()
    load.wait()

    @pl.when(part > 0)
    def _():
        to_next.wait_recv()

    @pl.when(part < parts - 1)
    def _():
        to_last.wait_recv()

    def near_copy(k):
        return along(
            totals.at[k, :, 1 - core],
            near.at[k],
            near_send.at[k],
            near_sem.at[k],
            part + 1 - 2 * core,
        )

    def far_copy(k, d):
        target = lax.rem(place + d, places)
        return along(
            near.at[k, target],
            far.at[k, d - 1],
            far_send.at[k, d - 1],
            far_sem.at[k, d - 1],
            target * 2 + core,
        )

    def pair_sum(k):
        near_copy(k).wait_recv()
        near[k] += totals[k, :, core]
        for d in range(1, places):
            far_copy(k, d).start()

    def add_product(k, held):
        product = lax.dot_general(
            held, lower[...], (((0,), (0,)), ((), ())), preferred_element_type=jnp.float32
        )
        totals[k] += product.reshape(totals.shape[1:])

    def fetch(c):
        first = pl.multiple_of(c * CHUNK, CHUNK)
        return pltpu.make_async_copy(lower_hbm.at[pl.ds(first, CHUNK)], lower, lower_sem)

    def up(c):
        return copy(own.at[c], from_two.at[c], send_up.at[c], two_sem.at[c], above)

    def across(c):
        return copy(own.at[c], from_one.at[c], send_across.at[c], one_sem.at[c], partner)

    def swap_odd(c):
        return copy(from_two.at[c], from_one.at[c], send_swap.at[c], one_sem.at[c], partner)

    def swap_even(c):
        return copy(from_two.at[c], from_three.at[c], send_swap.at[c], three_sem.at[c], partner)

    def second(c):
        return copy(from_one.at[c], from_three.at[c], send_second.at[c], three_sem.at[c], above)

    def passed(c):
        g = c // 3
        return copy(from_two.at[c], passing.at[g], send_passing.at[g], passing_sem.at[g], above)

    def last(c):
        g = c // 3
        return copy(passing.at[g], from_three.at[c], send_last.at[g], three_sem.at[c], partner)

    def make_image(c):
        for j in range(per_chunk):
            b = c * per_chunk + j
            stacked = jnp.concatenate([upper[b + 2], upper[b + 2 + offsets[b]]], axis=0)
            block = jnp.dot(dipole[b], stacked, preferred_element_type=jnp.float32)
            own[c, pl.ds(j * block_size, block_size), :] = block.astype(jnp.bfloat16)

    def body(t, carry):
        @pl.when(t < chunks)
        def _():
            make_image(t)
            up(t).start()

            @pl.when(is_even)
            def _():
                across(t).start()

        c = t - AHEAD

        @pl.when((c >= 0) & (c < chunks))
        def _():
            kind = lax.rem(c, 3)
            up(c).wait_recv()

            @pl.when(is_odd)
            def _():
                swap_odd(c).start()

            @pl.when(is_odd & (kind == 2))
            def _():
                passed(c).start()

            @pl.when(is_even & (kind != 0))
            def _():
                swap_even(c).start()

        b = t - AHEAD - 1

        @pl.when((b >= 0) & (b < chunks))
        def _():
            kind = lax.rem(b, 3)
            across(b).wait_recv()

            @pl.when((kind == 0) | (is_even & (kind == 1)))
            def _():
                second(b).start()

            fetch(b).start()
            fetch(b).wait()
            add_product(0, own[b])
            add_product(1, from_one[b])
            add_product(2, from_two[b])

        @pl.when(b == chunks - 1)
        def _():
            for k in range(STEPS - 1):
                near_copy(k).start()

        @pl.when(b == chunks)
        def _():
            for k in range(STEPS - 1):
                pair_sum(k)

        e = t - AHEAD - 2

        @pl.when((e >= 0) & (e < chunks) & is_odd & (lax.rem(e, 3) == 2))
        def _():
            passed(e).wait_recv()
            last(e).start()

        h = t - AHEAD - 3

        @pl.when((h >= 0) & (h < chunks))
        def _():
            fetch(h).start()
            second(h).wait_recv()
            fetch(h).wait()
            add_product(3, from_three[h])

        return carry

    lax.fori_loop(0, chunks + AHEAD + 3, body, 0)
    near_copy(STEPS - 1).start()
    pair_sum(STEPS - 1)

    def drain(c, carry):
        kind = lax.rem(c, 3)
        up(c).wait_send()

        @pl.when(is_even)
        def _():
            across(c).wait_send()

        @pl.when(is_odd)
        def _():
            swap_odd(c).wait_send()

        @pl.when(is_odd & (kind == 2))
        def _():
            passed(c).wait_send()
            last(c).wait_send()

        @pl.when(is_even & (kind != 0))
        def _():
            swap_even(c).wait_send()

        @pl.when((kind == 0) | (is_even & (kind == 1)))
        def _():
            second(c).wait_send()

        return carry

    lax.fori_loop(0, chunks, drain, 0)

    @pl.when(part < parts - 1)
    def _():
        to_next.wait_send()

    @pl.when(part > 0)
    def _():
        to_last.wait_send()

    labels_out[0] = labels[...]
    for k in range(1, STEPS):
        window(k).wait()
        labels_out[k] = windows[k - 1]
    for k in range(STEPS):
        near_copy(k).wait_send()
        total = near[k, place]
        for d in range(1, places):
            far_copy(k, d).wait()
            total = total + far[k, d - 1]
        out[k] = total


def moment_sums(states, parts, offsets, labels, upper_vectors, dipole_blocks, lower_vectors):
    rows, upper_count = upper_vectors.shape
    lower_count = lower_vectors.shape[1]
    block_size = dipole_blocks.shape[1]
    chunks = rows // CHUNK
    groups = (chunks + 2) // 3
    share = upper_count // parts
    places = parts // 2
    labels = jnp.broadcast_to(labels[None, :], (8, upper_count))
    held = pltpu.VMEM((chunks, CHUNK, upper_count), jnp.bfloat16)
    vmem = pl.BlockSpec(memory_space=pltpu.VMEM)
    hbm = pl.BlockSpec(memory_space=pl.ANY)
    dma = pltpu.SemaphoreType.DMA
    return pl.pallas_call(
        functools.partial(kernel, states, parts, chunks, block_size),
        out_shape=(
            jax.ShapeDtypeStruct((STEPS, share, lower_count), jnp.float32),
            jax.ShapeDtypeStruct((STEPS, 8, upper_count), jnp.int32),
        ),
        in_specs=[pl.BlockSpec(memory_space=pltpu.SMEM), vmem, hbm, vmem, hbm],
        out_specs=(vmem, vmem),
        scratch_shapes=[
            pltpu.VMEM((rows // block_size + 4, block_size, upper_count), jnp.bfloat16),
            held,
            held,
            held,
            held,
            pltpu.VMEM((groups, CHUNK, upper_count), jnp.bfloat16),
            pltpu.VMEM((CHUNK, lower_count), jnp.bfloat16),
            pltpu.VMEM((STEPS, places, 2, share, lower_count), jnp.float32),
            dma,
            dma,
            dma((chunks,)),
            dma((chunks,)),
            dma((chunks,)),
            dma((groups,)),
            dma((chunks,)),
            dma((chunks,)),
            dma((chunks,)),
            dma((chunks,)),
            dma((groups,)),
            dma((groups,)),
            pltpu.VMEM((STEPS - 1, 8, upper_count), jnp.int32),
            pltpu.VMEM((STEPS, places, share, lower_count), jnp.float32),
            pltpu.VMEM((STEPS, places - 1, share, lower_count), jnp.float32),
            dma((STEPS - 1,)),
            dma((STEPS - 1,)),
            dma((2,)),
            dma((2,)),
            dma((STEPS,)),
            dma((STEPS,)),
            dma((STEPS, places - 1)),
            dma((STEPS, places - 1)),
        ],
        compiler_params=pltpu.CompilerParams(
            collective_id=0, has_side_effects=True, vmem_limit_bytes=58 * 1024 * 1024
        ),
        cost_estimate=pl.CostEstimate(
            flops=2 * rows * upper_count * (STEPS * lower_count + 2 * block_size),
            bytes_accessed=2 * rows * (upper_count + lower_count + 2 * block_size),
            transcendentals=0,
        ),
    )(
        offsets,
        labels,
        upper_vectors.reshape(-1, block_size, upper_count),
        dipole_blocks,
        lower_vectors,
    )


def local(
    lower_vectors,
    upper_vectors,
    lower_labels,
    upper_labels,
    band_offsets,
    dipole_blocks,
    pair_table,
):
    states = lax.axis_size("state")
    basis = lax.axis_size("basis")
    summed, windows = moment_sums(
        states, basis, band_offsets, upper_labels, upper_vectors, dipole_blocks, lower_vectors
    )
    labels = windows[:, 0, :].T.reshape(-1)
    share = labels.shape[0] // basis
    labels = lax.dynamic_slice_in_dim(labels, lax.axis_index("basis") * share, share, 0)
    symbols = jnp.arange(pair_table.shape[0], dtype=jnp.int32)
    lower_onehot = (lower_labels[:, None] == symbols[None, :]).astype(jnp.float32)
    upper_onehot = (labels[:, None] == symbols[None, :]).astype(jnp.float32)
    allowed = jnp.dot(
        jnp.dot(lower_onehot, pair_table.astype(jnp.float32), precision=lax.Precision.HIGHEST),
        upper_onehot.T,
        precision=lax.Precision.HIGHEST,
    )
    norm_scale = float(lower_vectors.shape[0] * basis) ** (-0.5)
    summed = summed.transpose(2, 1, 0)
    return summed.reshape(allowed.shape) * allowed * norm_scale


def solution(mesh):
    return jax.shard_map(
        local,
        mesh=mesh,
        in_specs=(
            P("basis", "state"),
            P("basis", "state"),
            P("state"),
            P("state"),
            P("basis"),
            P("basis", None, None),
            P(),
        ),
        out_specs=P("state", "basis"),
        check_vma=False,
    )
```

```python
import functools

import jax
import jax.numpy as jnp
from jax import lax
from jax.experimental import pallas as pl
from jax.experimental.pallas import tpu as pltpu
from jax.sharding import PartitionSpec as P

STEPS = 4
CHUNK = 384
AHEAD = 2
LAGS = (1, 2, 4)
MESH = pl.DeviceIdType.MESH


def kernel(
    states,
    parts,
    chunks,
    block_size,
    offsets,
    labels,
    upper_hbm,
    dipole,
    lower_hbm,
    out,
    labels_out,
    upper,
    own,
    from_two,
    from_one,
    from_three,
    passing,
    lower,
    totals,
    load_sem,
    lower_sem,
    two_sem,
    one_sem,
    three_sem,
    passing_sem,
    send_up,
    send_across,
    send_swap,
    send_second,
    send_passing,
    send_last,
    windows,
    near,
    far,
    label_send,
    label_sem,
    halo_send,
    halo_sem,
    near_send,
    near_sem,
    far_send,
    far_sem,
):
    me = lax.axis_index("state")
    odd = lax.rem(me, 2)
    is_odd = odd == 1
    is_even = odd == 0
    partner = me + 1 - 2 * odd
    above = lax.rem(me + 2, states)
    below = lax.rem(me + states - 2, states)
    blocks = upper_hbm.shape[0]
    per_chunk = CHUNK // block_size

    part = lax.axis_index("basis")
    core = lax.rem(part, 2)
    place = part // 2
    places = parts // 2

    load = pltpu.make_async_copy(upper_hbm, upper.at[pl.ds(2, blocks)], load_sem)
    load.start()
    barrier = pltpu.get_barrier_semaphore()
    for step in range(1, STEPS):
        for other in (lax.rem(me + step, states), lax.rem(me + states - step, states)):
            pl.semaphore_signal(barrier, inc=1, device_id={"state": other}, device_id_type=MESH)
    for step in range(1, parts):
        other = lax.rem(part + step, parts)
        pl.semaphore_signal(barrier, inc=1, device_id={"basis": other}, device_id_type=MESH)
    edge = jnp.zeros((2,) + upper.shape[1:], upper.dtype)

    @pl.when(part == 0)
    def _():
        upper[pl.ds(0, 2)] = edge

    @pl.when(part == parts - 1)
    def _():
        upper[pl.ds(2 + blocks, 2)] = edge

    totals[...] = jnp.zeros_like(totals)
    pl.semaphore_wait(barrier, 2 * (STEPS - 1) + parts - 1)

    def along(source, target, send, receive, device):
        return pltpu.make_async_remote_copy(
            src_ref=source,
            dst_ref=target,
            send_sem=send,
            recv_sem=receive,
            device_id={"basis": device},
            device_id_type=MESH,
        )

    to_next = along(
        upper_hbm.at[pl.ds(blocks - 2, 2)],
        upper.at[pl.ds(0, 2)],
        halo_send.at[0],
        halo_sem.at[0],
        lax.rem(part + 1, parts),
    )
    to_last = along(
        upper_hbm.at[pl.ds(0, 2)],
        upper.at[pl.ds(2 + blocks, 2)],
        halo_send.at[1],
        halo_sem.at[1],
        lax.rem(part + parts - 1, parts),
    )

    @pl.when(part < parts - 1)
    def _():
        to_next.start()

    @pl.when(part > 0)
    def _():
        to_last.start()

    def copy(source, target, send, receive, device):
        return pltpu.make_async_remote_copy(
            src_ref=source,
            dst_ref=target,
            send_sem=send,
            recv_sem=receive,
            device_id={"state": device},
            device_id_type=MESH,
        )

    def window(k):
        return copy(
            labels,
            windows.at[k - 1],
            label_send.at[k - 1],
            label_sem.at[k - 1],
            lax.rem(me + k, states),
        )

    for k in range(1, STEPS):
        window(k).start()
    load.wait()

    @pl.when(part > 0)
    def _():
        to_next.wait_recv()

    @pl.when(part < parts - 1)
    def _():
        to_last.wait_recv()

    def near_copy(k):
        return along(
            totals.at[k, :, 1 - core],
            near.at[k],
            near_send.at[k],
            near_sem.at[k],
            part + 1 - 2 * core,
        )

    def far_copy(k, d):
        target = lax.rem(place + d, places)
        return along(
            near.at[k, target],
            far.at[k, d - 1],
            far_send.at[k, d - 1],
            far_sem.at[k, d - 1],
            target * 2 + core,
        )

    def pair_sum(k):
        near_copy(k).wait_recv()
        near[k] += totals[k, :, core]
        for d in range(1, places):
            far_copy(k, d).start()

    def add_product(k, held):
        product = lax.dot_general(
            held, lower[...], (((0,), (0,)), ((), ())), preferred_element_type=jnp.float32
        )
        totals[k] += product.reshape(totals.shape[1:])

    def fetch(c):
        first = pl.multiple_of(c * CHUNK, CHUNK)
        return pltpu.make_async_copy(lower_hbm.at[pl.ds(first, CHUNK)], lower, lower_sem)

    def up(c):
        return copy(own.at[c], from_two.at[c], send_up.at[c], two_sem.at[c], above)

    def across(c):
        return copy(own.at[c], from_one.at[c], send_across.at[c], one_sem.at[c], partner)

    def swap_odd(c):
        return copy(from_two.at[c], from_one.at[c], send_swap.at[c], one_sem.at[c], partner)

    def swap_even(c):
        return copy(from_two.at[c], from_three.at[c], send_swap.at[c], three_sem.at[c], partner)

    def second(c):
        return copy(from_one.at[c], from_three.at[c], send_second.at[c], three_sem.at[c], above)

    def passed(c):
        g = c // 3
        return copy(from_two.at[c], passing.at[g], send_passing.at[g], passing_sem.at[g], above)

    def last(c):
        g = c // 3
        return copy(passing.at[g], from_three.at[c], send_last.at[g], three_sem.at[c], partner)

    def make_image(c):
        for j in range(per_chunk):
            b = c * per_chunk + j
            stacked = jnp.concatenate([upper[b + 2], upper[b + 2 + offsets[b]]], axis=0)
            block = jnp.dot(dipole[b], stacked, preferred_element_type=jnp.float32)
            own[c, pl.ds(j * block_size, block_size), :] = block.astype(jnp.bfloat16)

    def body(t, carry):
        @pl.when(t < chunks)
        def _():
            make_image(t)
            up(t).start()

            @pl.when(is_even)
            def _():
                across(t).start()

        c = t - AHEAD

        @pl.when((c >= 0) & (c < chunks))
        def _():
            kind = lax.rem(c, 3)
            up(c).wait_recv()

            @pl.when(is_odd)
            def _():
                swap_odd(c).start()

            @pl.when(is_odd & (kind == 2))
            def _():
                passed(c).start()

            @pl.when(is_even & (kind != 0))
            def _():
                swap_even(c).start()

        b = t - AHEAD - LAGS[0]

        @pl.when((b >= 0) & (b < chunks))
        def _():
            kind = lax.rem(b, 3)
            across(b).wait_recv()

            @pl.when((kind == 0) | (is_even & (kind == 1)))
            def _():
                second(b).start()

            fetch(b).start()
            fetch(b).wait()
            add_product(0, own[b])
            add_product(1, from_one[b])
            add_product(2, from_two[b])

        @pl.when(b == chunks - 1)
        def _():
            for k in range(STEPS - 1):
                near_copy(k).start()

        @pl.when(b == chunks)
        def _():
            for k in range(STEPS - 1):
                pair_sum(k)

        e = t - AHEAD - LAGS[1]

        @pl.when((e >= 0) & (e < chunks) & is_odd & (lax.rem(e, 3) == 2))
        def _():
            passed(e).wait_recv()
            last(e).start()

        h = t - AHEAD - LAGS[2]

        @pl.when((h >= 0) & (h < chunks))
        def _():
            fetch(h).start()
            second(h).wait_recv()
            fetch(h).wait()
            add_product(3, from_three[h])

        return carry

    lax.fori_loop(0, chunks + AHEAD + max(LAGS[2], LAGS[0] + 1), body, 0)
    near_copy(STEPS - 1).start()
    pair_sum(STEPS - 1)

    def drain(c, carry):
        kind = lax.rem(c, 3)
        up(c).wait_send()

        @pl.when(is_even)
        def _():
            across(c).wait_send()

        @pl.when(is_odd)
        def _():
            swap_odd(c).wait_send()

        @pl.when(is_odd & (kind == 2))
        def _():
            passed(c).wait_send()
            last(c).wait_send()

        @pl.when(is_even & (kind != 0))
        def _():
            swap_even(c).wait_send()

        @pl.when((kind == 0) | (is_even & (kind == 1)))
        def _():
            second(c).wait_send()

        return carry

    lax.fori_loop(0, chunks, drain, 0)

    @pl.when(part < parts - 1)
    def _():
        to_next.wait_send()

    @pl.when(part > 0)
    def _():
        to_last.wait_send()

    labels_out[0] = labels[...]
    for k in range(1, STEPS):
        window(k).wait()
        labels_out[k] = windows[k - 1]
    for k in range(STEPS):
        near_copy(k).wait_send()
        total = near[k, place]
        for d in range(1, places):
            far_copy(k, d).wait()
            total = total + far[k, d - 1]
        out[k] = total


def moment_sums(states, parts, offsets, labels, upper_vectors, dipole_blocks, lower_vectors):
    rows, upper_count = upper_vectors.shape
    lower_count = lower_vectors.shape[1]
    block_size = dipole_blocks.shape[1]
    chunks = rows // CHUNK
    groups = (chunks + 2) // 3
    share = upper_count // parts
    places = parts // 2
    labels = jnp.broadcast_to(labels[None, :], (8, upper_count))
    held = pltpu.VMEM((chunks, CHUNK, upper_count), jnp.bfloat16)
    vmem = pl.BlockSpec(memory_space=pltpu.VMEM)
    hbm = pl.BlockSpec(memory_space=pl.ANY)
    dma = pltpu.SemaphoreType.DMA
    return pl.pallas_call(
        functools.partial(kernel, states, parts, chunks, block_size),
        out_shape=(
            jax.ShapeDtypeStruct((STEPS, share, lower_count), jnp.float32),
            jax.ShapeDtypeStruct((STEPS, 8, upper_count), jnp.int32),
        ),
        in_specs=[pl.BlockSpec(memory_space=pltpu.SMEM), vmem, hbm, vmem, hbm],
        out_specs=(vmem, vmem),
        scratch_shapes=[
            pltpu.VMEM((rows // block_size + 4, block_size, upper_count), jnp.bfloat16),
            held,
            held,
            held,
            held,
            pltpu.VMEM((groups, CHUNK, upper_count), jnp.bfloat16),
            pltpu.VMEM((CHUNK, lower_count), jnp.bfloat16),
            pltpu.VMEM((STEPS, places, 2, share, lower_count), jnp.float32),
            dma,
            dma,
            dma((chunks,)),
            dma((chunks,)),
            dma((chunks,)),
            dma((groups,)),
            dma((chunks,)),
            dma((chunks,)),
            dma((chunks,)),
            dma((chunks,)),
            dma((groups,)),
            dma((groups,)),
            pltpu.VMEM((STEPS - 1, 8, upper_count), jnp.int32),
            pltpu.VMEM((STEPS, places, share, lower_count), jnp.float32),
            pltpu.VMEM((STEPS, places - 1, share, lower_count), jnp.float32),
            dma((STEPS - 1,)),
            dma((STEPS - 1,)),
            dma((2,)),
            dma((2,)),
            dma((STEPS,)),
            dma((STEPS,)),
            dma((STEPS, places - 1)),
            dma((STEPS, places - 1)),
        ],
        compiler_params=pltpu.CompilerParams(
            collective_id=0, has_side_effects=True, vmem_limit_bytes=58 * 1024 * 1024
        ),
        cost_estimate=pl.CostEstimate(
            flops=2 * rows * upper_count * (STEPS * lower_count + 2 * block_size),
            bytes_accessed=2 * rows * (upper_count + lower_count + 2 * block_size),
            transcendentals=0,
        ),
    )(
        offsets,
        labels,
        upper_vectors.reshape(-1, block_size, upper_count),
        dipole_blocks,
        lower_vectors,
    )


def local(
    lower_vectors,
    upper_vectors,
    lower_labels,
    upper_labels,
    band_offsets,
    dipole_blocks,
    pair_table,
):
    states = lax.axis_size("state")
    basis = lax.axis_size("basis")
    summed, windows = moment_sums(
        states, basis, band_offsets, upper_labels, upper_vectors, dipole_blocks, lower_vectors
    )
    labels = windows[:, 0, :].T.reshape(-1)
    share = labels.shape[0] // basis
    labels = lax.dynamic_slice_in_dim(labels, lax.axis_index("basis") * share, share, 0)
    symbols = jnp.arange(pair_table.shape[0], dtype=jnp.int32)
    lower_onehot = (lower_labels[:, None] == symbols[None, :]).astype(jnp.float32)
    upper_onehot = (labels[:, None] == symbols[None, :]).astype(jnp.float32)
    allowed = jnp.dot(
        jnp.dot(lower_onehot, pair_table.astype(jnp.float32), precision=lax.Precision.HIGHEST),
        upper_onehot.T,
        precision=lax.Precision.HIGHEST,
    )
    norm_scale = float(lower_vectors.shape[0] * basis) ** (-0.5)
    summed = summed.transpose(2, 1, 0)
    return summed.reshape(allowed.shape) * allowed * norm_scale


def solution(mesh):
    return jax.shard_map(
        local,
        mesh=mesh,
        in_specs=(
            P("basis", "state"),
            P("basis", "state"),
            P("state"),
            P("state"),
            P("basis"),
            P("basis", None, None),
            P(),
        ),
        out_specs=P("state", "basis"),
        check_vma=False,
    )
```
